256 devices in a mesh: gx: 16 (over z_hi, y, core), gy: 16 (over z_lo, x).
Axes of the slice: x: 4, y: 4, z: 8 (z_hi: 2, z_lo: 4; z = z_hi * 4 + z_lo), core: 2. Of those that a mesh axis runs over, the one named last changes fastest.
Arguments:
- weights: bfloat16 [16384, 2, 64, 256], P(('gx', 'gy')), may hold values from -6 to 6
- slot_map: int32 [4, 64], replicated, may hold values from 0 to 63, each once within a row
- ops: bfloat16 [4, 4, 4, 2, 64, 64], replicated, may hold values from -0.25 to 0.25
- phase: float32 [4, 16384, 64], P(None, ('gx', 'gy')), may hold values from -3.140625 to 3.140625
Outputs:
- target_weights: bfloat16 [16384, 2, 64, 256], P(('gx', 'gy'))
The draws below stay inside these ranges and needn't reach their ends.
Inputs may be any that keep to these rules, and one draw needn't show every extreme that they name: Each row of slot_map is a permutation of 0 .. 63.
All inputs are finite; a program needn't handle non-finite values.
Results may differ from the reference program's by a relative error of at most 0.0064.
Values may be sent and summed in bfloat16 or wider, within the bound.
A program may use at most 128 MiB of HBM per device.

```python
import jax
import jax.numpy as jnp
from jax import lax

R = 64
RHS = 256
BLK = 64
LEVELS = 4
NB = 16384
N_GX = 16
N_GY = 16


def block_scale(own_key, extent, shards, least, top_value):
    def one(axis_at, blocks):
        steps = jax.random.uniform(jax.random.fold_in(jax.random.fold_in(own_key, 6), axis_at), (blocks,), jnp.float32, least / len(shards), top_value / len(shards))
        return jnp.repeat(jnp.exp(steps), extent[axis_at] // blocks).reshape((-1,) + (1,) * (len(extent) - axis_at - 1))

    factor_of = one(*shards[0])
    for cut in shards[1:]:
        factor_of = factor_of * one(*cut)
    return factor_of


def centred(own_key, extent, deviation, reach, shards=(), kind=jnp.bfloat16):
    level = block_scale(own_key, extent, shards, -0.22, 0.18) if shards else 1.0
    drawn = jax.random.normal(own_key, extent, jnp.float32) * deviation * level
    return jnp.minimum(jnp.maximum(drawn, -reach), reach).astype(kind)


def setup_inputs(seed: int = 0) -> dict:
    streams_of = jax.random.split(jax.random.key(seed), 5)
    return {
        "weights": centred(streams_of[0], (NB, 2, R, RHS), 1.0, 6.0, ((0, 256),)),
        "slot_map": jax.vmap(lambda own: jax.random.permutation(own, BLK))(jax.random.split(streams_of[1], LEVELS)).reshape((LEVELS, BLK)).astype(jnp.int32),
        "ops": centred(streams_of[2], (LEVELS, 4, 4, 2, R, R), (8 * R) ** -0.5, 0.25),
        "phase": jnp.clip(jax.random.uniform(streams_of[3], (LEVELS, NB, R), jnp.float32, -3.140625, 3.140625), -3.140625, 3.140625),
    }


def big_matrix(level_ops):
    real_part = level_ops[:, :, 0]
    imag_part = level_ops[:, :, 1]
    upper = jnp.stack([real_part, -imag_part], axis=2)
    lower = jnp.stack([imag_part, real_part], axis=2)
    full = jnp.stack([upper, lower], axis=2)
    full = jnp.transpose(full, (0, 2, 4, 1, 3, 5))
    size = full.shape[2]
    return full.reshape(8 * size, 8 * size)


def reference(weights, slot_map, ops, phase):
    groups = BLK // 4
    current = weights.reshape(N_GX, N_GY, BLK, 2, R, RHS)
    for level in range(LEVELS):
        on_gy = level % 2 == 1
        count = N_GY if on_gy else N_GX
        other = N_GX if on_gy else N_GY
        bit = count.bit_length() - 2 - level // 2
        ordered = jnp.take(current, slot_map[level].astype(jnp.int32), axis=2)
        angles = phase[level].reshape(N_GX, N_GY, BLK, R)
        if on_gy:
            ordered = jnp.swapaxes(ordered, 0, 1)
            angles = jnp.swapaxes(angles, 0, 1)
        outer = count >> (bit + 1)
        inner = 1 << bit
        viewed = ordered.reshape(outer, 2, inner, other, 2, groups, 2, 2, R, RHS)
        children = jnp.moveaxis(jnp.swapaxes(viewed, 1, 4), 4, 5)
        children = children.reshape(outer, 2, inner, other, groups, 8 * R, RHS)
        big = big_matrix(ops[level]).astype(jnp.float32)
        mixed = jnp.einsum('ij,abcdgjk->abcdgik', big, children.astype(jnp.float32), precision=lax.Precision.HIGHEST)
        mixed = mixed.reshape(outer, 2, inner, other, groups, 4, 2, R, RHS)
        angles = angles.reshape(outer, 2, inner, other, groups, 4, R)[..., None]
        cosine = jnp.cos(angles)
        sine = jnp.sin(angles)
        real_part = mixed[:, :, :, :, :, :, 0]
        imag_part = mixed[:, :, :, :, :, :, 1]
        rotated = jnp.stack([real_part * cosine - imag_part * sine, real_part * sine + imag_part * cosine], axis=6)
        rotated = rotated.astype(jnp.bfloat16).reshape(count, other, BLK, 2, R, RHS)
        if on_gy:
            rotated = jnp.swapaxes(rotated, 0, 1)
        current = rotated
    return current.reshape(N_GX * N_GY * BLK, 2, R, RHS)
```

```python
import functools

import jax
import jax.numpy as jnp
from jax import lax
from jax.experimental import pallas as pl
from jax.experimental.pallas import tpu as pltpu
from jax.sharding import PartitionSpec as P

MESH = pl.DeviceIdType.MESH
LEVELS = 4
PAIRS = 64
HALF = PAIRS // 2
GROUPS = PAIRS // 4
RANK = 64
ROWS = 2 * RANK
SIDES = 256
WIDE = 128
BIG = 4 * ROWS
PIECES = 4
PIECE = HALF // PIECES
CHUNKS = ((0, 32), (32, 32), (64, 32), (96, 32), (128, 32), (160, 32), (192, 32), (224, 16), (240, 16))
N_CHUNKS = len(CHUNKS)
FIRST = tuple(c for c in range(N_CHUNKS) if CHUNKS[c][0] < WIDE)
SECOND = tuple(c for c in range(N_CHUNKS) if CHUNKS[c][0] >= WIDE)
BLOCK = 8


def place():
    gx, gy = lax.axis_index("gx"), lax.axis_index("gy")
    sides, partners = [], []
    for level in range(LEVELS):
        axis, where = ("gy", gy) if level % 2 else ("gx", gx)
        step = lax.axis_size(axis) >> (1 + level // 2)
        side = (where // step) % 2
        other = where + step - 2 * step * side
        sides.append(side)
        partners.append((gx, other) if level % 2 else (other, gy))
    return sides, partners


def kernel(slots, weights, ops, phase, out, *scratch):
    w = scratch[0:2]
    ops_v, phase_v, matrix, turned, cosine, sine, cos3, sin3 = scratch[2:10]
    state = (None,) + scratch[10:13]
    sent0, got0 = scratch[13:15], scratch[15:17]
    result = scratch[17:19]
    rest = scratch[19:]
    sent = {}
    got = {}
    at = 0
    for level in range(1, LEVELS):
        for c in range(N_CHUNKS):
            sent[level, c], got[level, c] = rest[at], rest[at + 1]
            at += 2
    in_sem, out_sem, send0_sem, recv0_sem, send_sem, recv_sem = rest[at:]

    sides, partners = place()
    barrier = pltpu.get_barrier_semaphore()
    for partner in partners:
        pl.semaphore_signal(barrier, inc=1, device_id=partner, device_id_type=MESH)

    loads = [
        pltpu.make_async_copy(weights.at[:, :, pl.ds(half * WIDE, WIDE)], w[half], in_sem.at[half])
        for half in range(2)
    ]
    loads.append(pltpu.make_async_copy(ops, ops_v, in_sem.at[2]))
    loads.append(pltpu.make_async_copy(phase, phase_v, in_sem.at[3]))
    for load in loads:
        load.start()

    copies0 = {}
    for half in range(2):
        loads[half].wait()
        for piece in range(PIECES):

            @pl.loop(piece * PIECE, (piece + 1) * PIECE)
            def _(j, half=half):
                slot = slots[0, (1 - sides[0]) * HALF + j]
                sent0[half][j] = w[half][slot]

            if half == 0 and piece == 0:
                pl.semaphore_wait(barrier, LEVELS)
            rows = pl.ds(piece * PIECE, PIECE)
            copy = pltpu.make_async_remote_copy(
                src_ref=sent0[half].at[rows],
                dst_ref=got0[half].at[rows],
                send_sem=send0_sem.at[half, piece],
                recv_sem=recv0_sem.at[half, piece],
                device_id=partners[0],
                device_id_type=MESH,
            )
            copy.start()
            copies0[half, piece] = copy

    loads[2].wait()
    loads[3].wait()
    for level in range(LEVELS):
        for c in range(4):
            child = lax.rem(2 * sides[level] + c, 4)

            @pl.loop(0, 4)
            def _(q, level=level, c=c, child=child):
                real = ops_v[level, q, child, 0]
                imag = ops_v[level, q, child, 1]
                block = jnp.concatenate(
                    [jnp.concatenate([real, -imag], axis=1), jnp.concatenate([imag, real], axis=1)], axis=0
                )
                if level == LEVELS - 1:
                    matrix[pl.ds(q * ROWS, ROWS), pl.ds(c * ROWS, ROWS)] = block
                else:
                    turned[level, q, pl.ds(c * ROWS, ROWS), :] = block.T

        angles = phase_v[level]
        if level < LEVELS - 1:
            cos_l, sin_l = jnp.cos(angles), jnp.sin(angles)
            cosine[level] = jnp.concatenate([cos_l, cos_l], axis=1)
            sine[level] = jnp.concatenate([-sin_l, sin_l], axis=1)
        else:
            flat = angles.T
            cos_l, sin_l = jnp.cos(flat), jnp.sin(flat)
            for i in range(PAIRS):
                cos3[i] = jnp.broadcast_to(cos_l[:, i : i + 1], (RANK, WIDE))
                sin3[i] = jnp.broadcast_to(sin_l[:, i : i + 1], (RANK, WIDE))

    def rotate(level, pair, z):
        c = cosine[level, pl.ds(pair, 1), :]
        s = sine[level, pl.ds(pair, 1), :]
        return (z * c + pltpu.roll(z, RANK, 1) * s).astype(jnp.bfloat16)

    def mix(level, columns):
        return [
            jnp.dot(columns, turned[level, q], preferred_element_type=jnp.float32) for q in range(4)
        ]

    def first_level(half, piece):
        copies0[half, piece].wait_recv()

        @pl.loop(piece * PIECE // 2, (piece + 1) * PIECE // 2, step=2)
        def _(g0):
            stack = []
            for k in range(2):
                g = g0 + k
                tiles = [w[half][slots[0, sides[0] * HALF + 2 * g + e]].T for e in range(2)]
                tiles += [got0[half][2 * g + e].T for e in range(2)]
                stack.append(jnp.concatenate(tiles, axis=1))
            z = mix(0, jnp.concatenate(stack, axis=0))
            for k in range(2):
                for q in range(4):
                    pair = (g0 + k) * 4 + q
                    state[1][pair, pl.ds(half * WIDE, WIDE), :] = rotate(0, pair, z[q][k * WIDE : (k + 1) * WIDE])

    copies = {}

    def send(level, c):
        start, width = CHUNKS[c]

        @pl.loop(0, HALF, unroll=4)
        def _(j):
            slot = slots[level, (1 - sides[level]) * HALF + j]
            sent[level, c][j] = state[level][slot, pl.ds(start, width), :]

        copy = pltpu.make_async_remote_copy(
            src_ref=sent[level, c],
            dst_ref=got[level, c],
            send_sem=send_sem.at[level - 1, c],
            recv_sem=recv_sem.at[level - 1, c],
            device_id=partners[level],
            device_id_type=MESH,
        )
        copy.start()
        copies[level, c] = copy

    def middle_level(level, c):
        start, width = CHUNKS[c]
        copies[level, c].wait_recv()

        @pl.loop(0, GROUPS, step=BLOCK)
        def _(g0):
            stack = []
            for k in range(BLOCK):
                g = g0 + k
                tiles = [
                    state[level][slots[level, sides[level] * HALF + 2 * g + e], pl.ds(start, width), :]
                    for e in range(2)
                ]
                tiles += [got[level, c][2 * g + e] for e in range(2)]
                stack.append(jnp.concatenate(tiles, axis=1))
            z = mix(level, jnp.concatenate(stack, axis=0))
            for k in range(BLOCK):
                for q in range(4):
                    pair = (g0 + k) * 4 + q
                    state[level + 1][pair, pl.ds(start, width), :] = rotate(
                        level, pair, z[q][k * width : (k + 1) * width]
                    )

    stores = []

    def last_level(half):
        level = LEVELS - 1
        chunks = SECOND if half else FIRST
        for c in chunks:
            copies[level, c].wait_recv()

        @pl.loop(0, GROUPS, step=2)
        def _(g0):
            stack = []
            for k in range(2):
                g = g0 + k
                tiles = [
                    state[level][slots[level, sides[level] * HALF + 2 * g + e], pl.ds(half * WIDE, WIDE), :]
                    for e in range(2)
                ]
                tiles += [jnp.concatenate([got[level, c][2 * g + e] for c in chunks], axis=0) for e in range(2)]
                stack.append(jnp.concatenate(tiles, axis=1))
            z = lax.dot_general(
                matrix[...],
                jnp.concatenate(stack, axis=0),
                (((1,), (1,)), ((), ())),
                preferred_element_type=jnp.float32,
            )
            for k in range(2):
                for q in range(4):
                    pair = (g0 + k) * 4 + q
                    lanes = slice(k * WIDE, (k + 1) * WIDE)
                    real = z[q * ROWS : q * ROWS + RANK, lanes]
                    imag = z[q * ROWS + RANK : (q + 1) * ROWS, lanes]
                    c, s = cos3[pair], sin3[pair]
                    result[half][pair, :RANK, :] = (real * c - imag * s).astype(jnp.bfloat16)
                    result[half][pair, RANK:, :] = (real * s + imag * c).astype(jnp.bfloat16)

        store = pltpu.make_async_copy(result[half], out.at[:, :, pl.ds(half * WIDE, WIDE)], out_sem.at[half])
        store.start()
        stores.append(store)

    def run(*steps):
        for what, c in steps:
            if what in "123":
                send(int(what), c)
            elif what in "ab":
                middle_level("ab".index(what) + 1, c)

    for piece in range(PIECES):
        first_level(0, piece)
    run(("1", 0), ("1", 1))
    first_level(1, 0)
    run(("a", 0), ("2", 0))
    first_level(1, 1)
    run(("a", 1), ("2", 1), ("b", 0), ("3", 0))
    first_level(1, 2)
    run(("1", 2))
    first_level(1, 3)
    run(("1", 3), *(("1", c) for c in SECOND))
    run(("b", 1), ("3", 1))
    late = list(range(2, N_CHUNKS))
    for n, c in enumerate(late):
        run(("a", c), ("2", c))
        if n >= 1:
            run(("b", late[n - 1]), ("3", late[n - 1]))
        if c == late[4]:
            last_level(0)
    run(("b", late[-1]), ("3", late[-1]))
    last_level(1)

    for store in stores:
        store.wait()
    for copy in copies0.values():
        copy.wait_send()
    for copy in copies.values():
        copy.wait_send()


def on_device(weights, slot_map, ops, phase):
    hbm = pl.BlockSpec(memory_space=pl.ANY)
    bf16, f32 = jnp.bfloat16, jnp.float32
    scratch = [pltpu.VMEM((PAIRS, ROWS, WIDE), bf16)] * 2
    scratch += [
        pltpu.VMEM(ops.shape, bf16),
        pltpu.VMEM(phase.shape, f32),
        pltpu.VMEM((BIG, BIG), bf16),
        pltpu.VMEM((LEVELS - 1, 4, BIG, ROWS), bf16),
        pltpu.VMEM((LEVELS - 1, PAIRS, ROWS), f32),
        pltpu.VMEM((LEVELS - 1, PAIRS, ROWS), f32),
        pltpu.VMEM((PAIRS, RANK, WIDE), f32),
        pltpu.VMEM((PAIRS, RANK, WIDE), f32),
    ]
    scratch += [pltpu.VMEM((PAIRS, SIDES, ROWS), bf16)] * (LEVELS - 1)
    scratch += [pltpu.VMEM((HALF, ROWS, WIDE), bf16)] * 4
    scratch += [pltpu.VMEM((PAIRS, ROWS, WIDE), bf16)] * 2
    for _ in range(1, LEVELS):
        for _, width in CHUNKS:
            scratch += [pltpu.VMEM((HALF, width, ROWS), bf16)] * 2
    scratch += [
        pltpu.SemaphoreType.DMA((4,)),
        pltpu.SemaphoreType.DMA((2,)),
        pltpu.SemaphoreType.DMA((2, PIECES)),
        pltpu.SemaphoreType.DMA((2, PIECES)),
        pltpu.SemaphoreType.DMA((LEVELS - 1, N_CHUNKS)),
        pltpu.SemaphoreType.DMA((LEVELS - 1, N_CHUNKS)),
    ]
    out = pl.pallas_call(
        kernel,
        out_shape=jax.ShapeDtypeStruct((PAIRS, ROWS, SIDES), bf16),
        in_specs=[pl.BlockSpec(memory_space=pltpu.SMEM), hbm, hbm, hbm],
        out_specs=hbm,
        scratch_shapes=scratch,
        compiler_params=pltpu.CompilerParams(
            collective_id=0, has_side_effects=True, vmem_limit_bytes=60 * 2**20
        ),
        cost_estimate=pl.CostEstimate(flops=8_600_000_000, bytes_accessed=10_000_000, transcendentals=0),
    )(slot_map, weights.reshape(PAIRS, ROWS, SIDES), ops, phase)
    return out.reshape(weights.shape)


def solution(mesh):
    placed = (P(("gx", "gy"), None, None, None), P(), P(), P(None, ("gx", "gy"), None))
    return jax.shard_map(
        on_device,
        mesh=mesh,
        in_specs=placed,
        out_specs=P(("gx", "gy"), None, None, None),
        check_vma=False,
    )
```

```python
import jax
import jax.numpy as jnp
from jax import lax
from jax.experimental import pallas as pl
from jax.experimental.pallas import tpu as pltpu
from jax.sharding import PartitionSpec as P

MESH = pl.DeviceIdType.MESH
LEVELS = 4
PAIRS = 64
HALF = PAIRS // 2
GROUPS = PAIRS // 4
RANK = 64
ROWS = 2 * RANK
SIDES = 256
WIDE = 128
BIG = 4 * ROWS
PIECES = 4
PIECE = HALF // PIECES
WIDTHS = (16, 16, 16, 16, 32, 32)
STARTS = tuple(sum(WIDTHS[:c]) for c in range(len(WIDTHS)))
CHUNKS = len(WIDTHS)
LAST = CHUNKS - 1
WINDOW = 2
LAG = 1
PLAIN, CROSSED = 0, 1


class Place:
    def __init__(self):
        gx, gy = lax.axis_index("gx"), lax.axis_index("gy")
        self.sides, self.partners = [], []
        for level in range(LEVELS):
            axis, where = ("gy", gy) if level % 2 else ("gx", gx)
            step = lax.axis_size(axis) >> (1 + level // 2)
            side = (where // step) % 2
            other = where + step - 2 * step * side
            self.sides.append(side)
            self.partners.append((gx, other) if level % 2 else (other, gy))
        far, near = lax.axis_size("gy") >> 1, lax.axis_size("gy") >> 2
        self.high, self.low = self.sides[1], self.sides[3]
        rest = gy % near
        self.moves = self.high != self.low
        crossed = self.low * far + self.high * near + rest
        self.crossed = (gx, crossed)
        self.crossed_partner = (self.partners[0][0], crossed)
        self.homes = [(gx, self.low * far + u * near + rest) for u in range(2)]

    def stays(self, u):
        return (self.high == u) & (self.low == u)


def kernel(slots, weights, ops, phase, out, *scratch):
    w, scratch = scratch[0:2], scratch[2:]
    ops_v, phase_v, angles_out, angles_in, matrix, turned, cosine, sine, cos3, sin3 = scratch[:10]
    state = (None,) + scratch[10:13]
    sent0, got0, sent_kept, got_kept = scratch[13:15], scratch[15:17], scratch[17], scratch[18]
    result = scratch[19:21]
    rest = scratch[21:]
    sent, got = {}, {}
    at = 0
    for level in range(1, LEVELS):
        for half in range(2):
            for c in range(CHUNKS):
                sent[level, half, c], got[level, half, c] = rest[at], rest[at + 1]
                at += 2
    in_sem, out_sem, send0_sem, recv0_sem, angle_sem, send_sem, recv_sem, home_send_sem, home_recv_sem = rest[at:]

    here = Place()
    sides, partners = here.sides, here.partners
    barrier = pltpu.get_barrier_semaphore()
    for partner in partners:
        pl.semaphore_signal(barrier, inc=1, device_id=partner, device_id_type=MESH)

    @pl.when(here.moves)
    def _():
        for partner in (here.crossed, here.crossed_partner):
            pl.semaphore_signal(barrier, inc=1, device_id=partner, device_id_type=MESH)

    loads = [
        pltpu.make_async_copy(weights.at[:, :, pl.ds(half * WIDE, WIDE)], w[half], in_sem.at[half])
        for half in range(2)
    ]
    loads.append(pltpu.make_async_copy(phase, phase_v, in_sem.at[2]))
    loads.append(pltpu.make_async_copy(ops, ops_v, in_sem.at[3]))
    for load in loads:
        load.start()

    def remote(src, dst, send, recv, target):
        return pltpu.make_async_remote_copy(
            src_ref=src, dst_ref=dst, send_sem=send, recv_sem=recv, device_id=target, device_id_type=MESH
        )

    def other_copy(half, piece):
        rows = pl.ds(piece * PIECE, PIECE)
        target = here.crossed_partner if half == CROSSED else partners[0]
        return remote(
            sent0[half].at[rows], got0[half].at[rows], send0_sem.at[half, piece], recv0_sem.at[half, piece], target
        )

    def kept_copy(piece):
        rows = pl.ds(piece * PIECE, PIECE)
        return remote(
            sent_kept.at[rows], got_kept.at[rows], send0_sem.at[2, piece], recv0_sem.at[2, piece], here.crossed
        )

    def angle_copy():
        return remote(angles_out, angles_in, angle_sem.at[0], angle_sem.at[1], here.crossed)

    def pick(half, side, piece, dst):
        @pl.loop(piece * PIECE, (piece + 1) * PIECE)
        def _(j):
            dst[j] = w[half][slots[0, side * HALF + j]]

    for half in range(2):
        loads[half].wait()
        for piece in range(PIECES):
            pick(half, 1 - sides[0], piece, sent0[half])
            if half == 0 and piece == 0:
                pl.semaphore_wait(barrier, LEVELS + 2 * (here.high + here.low - 2 * here.high * here.low))

            other_copy(half, piece).start()
            if half == CROSSED:

                @pl.when(here.moves)
                def _(piece=piece):
                    pick(CROSSED, sides[0], piece, sent_kept)
                    kept_copy(piece).start()

                @pl.when(jnp.logical_not(here.moves))
                def _(piece=piece):
                    pick(CROSSED, sides[0], piece, got_kept)

    loads[2].wait()
    for level in range(LEVELS - 1):
        angles_out[level] = jnp.concatenate([phase_v[level, :HALF], phase_v[level, HALF:]], axis=1)

    @pl.when(here.moves)
    def _():
        angle_copy().start()

    @pl.when(jnp.logical_not(here.moves))
    def _():
        angles_in[...] = angles_out[...]

    loads[3].wait()
    for level, side, into in (
        (0, sides[0], 0),
        (1, sides[1], 1),
        (2, sides[2], 2),
        (1, sides[3], 3),
        (3, sides[3], None),
        (3, None, None),
    ):
        for c in range(4):
            child = c if side is None else lax.rem(2 * side + c, 4)

            @pl.loop(0, 4)
            def _(q, level=level, side=side, into=into, c=c, child=child):
                real = ops_v[level, q, child, 0]
                imag = ops_v[level, q, child, 1]
                block = jnp.concatenate(
                    [jnp.concatenate([real, -imag], axis=1), jnp.concatenate([imag, real], axis=1)], axis=0
                )
                if into is None:
                    order = CROSSED if side is None else PLAIN
                    matrix[order, pl.ds(q * ROWS, ROWS), pl.ds(c * ROWS, ROWS)] = block
                else:
                    turned[into, q, pl.ds(c * ROWS, ROWS), :] = block.T

    def factors(half, level, angles):
        cos_l, sin_l = jnp.cos(angles), jnp.sin(angles)
        cosine[half, level] = jnp.concatenate([cos_l, cos_l], axis=1)
        sine[half, level] = jnp.concatenate([-sin_l, sin_l], axis=1)

    for level in range(LEVELS - 1):
        factors(PLAIN, level, phase_v[level])
    flat = phase_v[LEVELS - 1].T
    cos_l, sin_l = jnp.cos(flat), jnp.sin(flat)
    for i in range(PAIRS):
        cos3[i] = jnp.broadcast_to(cos_l[:, i : i + 1], (RANK, WIDE))
        sin3[i] = jnp.broadcast_to(sin_l[:, i : i + 1], (RANK, WIDE))

    def rotate(half, level, pair, z):
        c = cosine[half, level, pl.ds(pair, 1), :]
        s = sine[half, level, pl.ds(pair, 1), :]
        return (z * c + pltpu.roll(z, RANK, 1) * s).astype(jnp.bfloat16)

    def mix(which, columns):
        return [
            jnp.dot(columns, turned[which, q], preferred_element_type=jnp.float32) for q in range(4)
        ]

    def first_level(half, piece):
        other_copy(half, piece).wait_recv()
        if half == CROSSED:

            @pl.when(here.moves)
            def _():
                kept_copy(piece).wait_recv()

        @pl.loop(piece * PIECE // 2, (piece + 1) * PIECE // 2, step=2)
        def _(g0):
            stack = []
            for k in range(2):
                g = g0 + k
                if half == CROSSED:
                    tiles = [got_kept[2 * g + e].T for e in range(2)]
                else:
                    tiles = [w[half][slots[0, sides[0] * HALF + 2 * g + e]].T for e in range(2)]
                tiles += [got0[half][2 * g + e].T for e in range(2)]
                stack.append(jnp.concatenate(tiles, axis=1))
            z = mix(0, jnp.concatenate(stack, axis=0))
            for k in range(2):
                for q in range(4):
                    pair = (g0 + k) * 4 + q
                    state[1][pair, pl.ds(half * WIDE, WIDE), :] = rotate(
                        half, 0, pair, z[q][k * WIDE : (k + 1) * WIDE]
                    )

    def hop(level, half):
        return 3 if level == 1 and half == CROSSED else level

    def parts(level, c):
        if level == LEVELS - 1 and c == LAST:
            return [pl.ds(piece * PIECE, PIECE) for piece in range(PIECES)]
        return [pl.ds(0, HALF)]

    def chunk_copy(level, half, c, n):
        rows, at = parts(level, c)[n], hop(level, half)
        return remote(
            sent[level, half, c].at[rows],
            got[level, half, c].at[rows],
            send_sem.at[level - 1, half, c, n],
            recv_sem.at[level - 1, half, c, n],
            partners[at],
        )

    def home_copy(c, n, u, slot):
        rows = parts(LEVELS - 1, c)[n]
        return remote(
            sent[LEVELS - 1, CROSSED, c].at[u, rows],
            got[LEVELS - 1, CROSSED, c].at[slot, rows],
            home_send_sem.at[u, c, n],
            home_recv_sem.at[slot, c, n],
            here.homes[u],
        )

    started = []

    def send(level, half, c):
        if c >= CHUNKS:
            return
        columns = pl.ds(half * WIDE + STARTS[c], WIDTHS[c])

        def gather(side, rows, put):
            @pl.loop(rows.start, rows.start + rows.size, unroll=4)
            def _(j):
                put(j, state[level][slots[level, side * HALF + j], columns, :])

        for n, rows in enumerate(parts(level, c)):
            if level < LEVELS - 1 or half == PLAIN:

                def put(j, tile):
                    sent[level, half, c][j] = tile

                gather(1 - sides[hop(level, half)], rows, put)
                chunk_copy(level, half, c, n).start()
                started.append((level, half, c, n))
                continue
            for u in range(2):

                @pl.when(here.stays(u))
                def _(u=u, rows=rows):
                    def put(j, tile):
                        got[level, half, c][u, j] = tile

                    gather(u, rows, put)

                @pl.when(jnp.logical_not(here.stays(u)))
                def _(u=u, rows=rows, n=n):
                    def put(j, tile):
                        sent[level, half, c][u, j] = tile

                    gather(u, rows, put)
                    home_copy(c, n, u, here.high).start()

    def middle_level(level, half, c):
        width, block = WIDTHS[c], 256 // WIDTHS[c]
        columns = pl.ds(half * WIDE + STARTS[c], width)
        side = sides[hop(level, half)]
        which = 3 if level == 1 and half == CROSSED else level

        @pl.loop(0, GROUPS, step=block)
        def _(g0):
            stack = []
            for k in range(block):
                g = g0 + k
                tiles = [state[level][slots[level, side * HALF + 2 * g + e], columns, :] for e in range(2)]
                tiles += [got[level, half, c][2 * g + e] for e in range(2)]
                stack.append(jnp.concatenate(tiles, axis=1))
            z = mix(which, jnp.concatenate(stack, axis=0))
            for k in range(block):
                for q in range(4):
                    pair = (g0 + k) * 4 + q
                    state[level + 1][pair, columns, :] = rotate(half, level, pair, z[q][k * width : (k + 1) * width])

    stores = []

    def last_level(half, piece):
        level = LEVELS - 1
        for c in range(CHUNKS):
            n = piece if c == LAST else 0
            if c < LAST and piece > 0:
                continue
            if half == PLAIN:
                chunk_copy(level, half, c, n).wait_recv()
                continue
            for s in range(2):

                @pl.when(jnp.logical_not(here.stays(s)))
                def _(c=c, n=n, s=s):
                    home_copy(c, n, 0, s).wait_recv()

        @pl.loop(piece * GROUPS // PIECES, (piece + 1) * GROUPS // PIECES, step=2)
        def _(g0):
            stack = []
            for k in range(2):
                g = g0 + k
                if half == PLAIN:
                    tiles = [
                        state[level][slots[level, sides[level] * HALF + 2 * g + e], pl.ds(half * WIDE, WIDE), :]
                        for e in range(2)
                    ]
                    tiles += [
                        jnp.concatenate([got[level, half, c][2 * g + e] for c in range(CHUNKS)], axis=0)
                        for e in range(2)
                    ]
                else:
                    tiles = [
                        jnp.concatenate([got[level, half, c][s, 2 * g + e] for c in range(CHUNKS)], axis=0)
                        for s in range(2)
                        for e in range(2)
                    ]
                stack.append(jnp.concatenate(tiles, axis=1))
            z = lax.dot_general(
                matrix[half],
                jnp.concatenate(stack, axis=0),
                (((1,), (1,)), ((), ())),
                preferred_element_type=jnp.float32,
            )
            for k in range(2):
                for q in range(4):
                    pair = (g0 + k) * 4 + q
                    lanes = slice(k * WIDE, (k + 1) * WIDE)
                    real = z[q * ROWS : q * ROWS + RANK, lanes]
                    imag = z[q * ROWS + RANK : (q + 1) * ROWS, lanes]
                    c, s = cos3[pair], sin3[pair]
                    result[half][pair, :RANK, :] = (real * c - imag * s).astype(jnp.bfloat16)
                    result[half][pair, RANK:, :] = (real * s + imag * c).astype(jnp.bfloat16)

        pairs = pl.ds(piece * PAIRS // PIECES, PAIRS // PIECES)
        store = pltpu.make_async_copy(
            result[half].at[pairs], out.at[pairs, :, pl.ds(half * WIDE, WIDE)], out_sem.at[half, piece]
        )
        store.start()
        stores.append(store)

    def take(level, half, c):
        chunk_copy(level, half, c, 0).wait_recv()
        if level == 1:
            send(1, half, c + WINDOW)
        middle_level(level, half, c)
        send(level + 1, half, c)

    for piece in range(PIECES):
        first_level(PLAIN, piece)

    @pl.when(here.moves)
    def _():
        angle_copy().wait_recv()

    for level in range(LEVELS - 1):
        packed = angles_in[level]
        factors(CROSSED, level, jnp.concatenate([packed[:, :RANK], packed[:, RANK:]], axis=0))
    for piece in range(PIECES):
        first_level(CROSSED, piece)
        if piece == PIECES - 2:
            for c in range(WINDOW):
                send(1, PLAIN, c)
    for c in range(WINDOW):
        send(1, CROSSED, c)
    for c in range(CHUNKS + LAG):
        if c < CHUNKS:
            take(1, PLAIN, c)
            take(1, CROSSED, c)
        if c >= LAG:
            take(2, PLAIN, c - LAG)
            take(2, CROSSED, c - LAG)
    for piece in range(PIECES):
        last_level(PLAIN, piece)
        last_level(CROSSED, piece)

    for store in stores:
        store.wait()
    for half in range(2):
        for piece in range(PIECES):
            other_copy(half, piece).wait_send()
    for key in started:
        chunk_copy(*key).wait_send()

    @pl.when(here.moves)
    def _():
        angle_copy().wait_send()
        for piece in range(PIECES):
            kept_copy(piece).wait_send()

    for u in range(2):

        @pl.when(jnp.logical_not(here.stays(u)))
        def _(u=u):
            for c in range(CHUNKS):
                for n in range(len(parts(LEVELS - 1, c))):
                    home_copy(c, n, u, 0).wait_send()


def on_device(weights, slot_map, ops, phase):
    hbm = pl.BlockSpec(memory_space=pl.ANY)
    bf16, f32 = jnp.bfloat16, jnp.float32
    scratch = [pltpu.VMEM((PAIRS, ROWS, WIDE), bf16)] * 2
    scratch += [
        pltpu.VMEM(ops.shape, bf16),
        pltpu.VMEM(phase.shape, f32),
        pltpu.VMEM((LEVELS - 1, HALF, ROWS), f32),
        pltpu.VMEM((LEVELS - 1, HALF, ROWS), f32),
        pltpu.VMEM((2, BIG, BIG), bf16),
        pltpu.VMEM((4, 4, BIG, ROWS), bf16),
        pltpu.VMEM((2, LEVELS - 1, PAIRS, ROWS), f32),
        pltpu.VMEM((2, LEVELS - 1, PAIRS, ROWS), f32),
        pltpu.VMEM((PAIRS, RANK, WIDE), f32),
        pltpu.VMEM((PAIRS, RANK, WIDE), f32),
    ]
    scratch += [pltpu.VMEM((PAIRS, SIDES, ROWS), bf16)] * (LEVELS - 1)
    scratch += [pltpu.VMEM((HALF, ROWS, WIDE), bf16)] * 6
    scratch += [pltpu.VMEM((PAIRS, ROWS, WIDE), bf16)] * 2
    for level in range(1, LEVELS):
        for half in range(2):
            for width in WIDTHS:
                shape = (HALF, width, ROWS)
                if level == LEVELS - 1 and half == CROSSED:
                    shape = (2,) + shape
                scratch += [pltpu.VMEM(shape, bf16)] * 2
    scratch += [
        pltpu.SemaphoreType.DMA((4,)),
        pltpu.SemaphoreType.DMA((2, PIECES)),
        pltpu.SemaphoreType.DMA((3, PIECES)),
        pltpu.SemaphoreType.DMA((3, PIECES)),
        pltpu.SemaphoreType.DMA((2,)),
        pltpu.SemaphoreType.DMA((LEVELS - 1, 2, CHUNKS, PIECES)),
        pltpu.SemaphoreType.DMA((LEVELS - 1, 2, CHUNKS, PIECES)),
        pltpu.SemaphoreType.DMA((2, CHUNKS, PIECES)),
        pltpu.SemaphoreType.DMA((2, CHUNKS, PIECES)),
    ]
    out = pl.pallas_call(
        kernel,
        out_shape=jax.ShapeDtypeStruct((PAIRS, ROWS, SIDES), bf16),
        in_specs=[pl.BlockSpec(memory_space=pltpu.SMEM), hbm, hbm, hbm],
        out_specs=hbm,
        scratch_shapes=scratch,
        compiler_params=pltpu.CompilerParams(
            collective_id=0, has_side_effects=True, vmem_limit_bytes=60 * 2**20
        ),
        cost_estimate=pl.CostEstimate(flops=8_600_000_000, bytes_accessed=10_000_000, transcendentals=0),
    )(slot_map, weights.reshape(PAIRS, ROWS, SIDES), ops, phase)
    return out.reshape(weights.shape)


def solution(mesh):
    placed = (P(("gx", "gy"), None, None, None), P(), P(), P(None, ("gx", "gy"), None))
    return jax.shard_map(
        on_device,
        mesh=mesh,
        in_specs=placed,
        out_specs=P(("gx", "gy"), None, None, None),
        check_vma=False,
    )
```

```python
import jax
import jax.numpy as jnp
from jax import lax
from jax.experimental import pallas as pl
from jax.experimental.pallas import tpu as pltpu
from jax.sharding import PartitionSpec as P

MESH = pl.DeviceIdType.MESH
LEVELS = 4
PAIRS = 64
HALF = PAIRS // 2
GROUPS = PAIRS // 4
RANK = 64
ROWS = 2 * RANK
SIDES = 256
WIDE = 128
BIG = 4 * ROWS
PIECES = 4
PIECE = HALF // PIECES
WIDTHS = (16, 16, 16, 32, 32, 16)
STARTS = tuple(sum(WIDTHS[:c]) for c in range(len(WIDTHS)))
CHUNKS = len(WIDTHS)
LAST = CHUNKS - 1
WINDOW = 2
LAG = 1
PLAIN, CROSSED = 0, 1


class Place:
    def __init__(self):
        gx, gy = lax.axis_index("gx"), lax.axis_index("gy")
        self.sides, self.partners = [], []
        for level in range(LEVELS):
            axis, where = ("gy", gy) if level % 2 else ("gx", gx)
            step = lax.axis_size(axis) >> (1 + level // 2)
            side = (where // step) % 2
            other = where + step - 2 * step * side
            self.sides.append(side)
            self.partners.append((gx, other) if level % 2 else (other, gy))
        far, near = lax.axis_size("gy") >> 1, lax.axis_size("gy") >> 2
        self.high, self.low = self.sides[1], self.sides[3]
        rest = gy % near
        self.moves = self.high != self.low
        crossed = self.low * far + self.high * near + rest
        self.crossed = (gx, crossed)
        self.crossed_partner = (self.partners[0][0], crossed)
        self.homes = [(gx, self.low * far + u * near + rest) for u in range(2)]

    def stays(self, u):
        return (self.high == u) & (self.low == u)


def kernel(slots, weights, ops, phase, out, *scratch):
    w, scratch = scratch[0:2], scratch[2:]
    ops_v, phase_v, angles_out, angles_in, matrix, turned, cosine, sine, cos3, sin3 = scratch[:10]
    state = (None,) + scratch[10:13]
    sent0, got0, sent_kept, got_kept = scratch[13:15], scratch[15:17], scratch[17], scratch[18]
    result = scratch[19:21]
    rest = scratch[21:]
    sent, got = {}, {}
    at = 0
    for level in range(1, LEVELS):
        for half in range(2):
            for c in range(CHUNKS):
                sent[level, half, c], got[level, half, c] = rest[at], rest[at + 1]
                at += 2
    in_sem, out_sem, send0_sem, recv0_sem, angle_sem, send_sem, recv_sem, home_send_sem, home_recv_sem = rest[at:]

    here = Place()
    sides, partners = here.sides, here.partners
    barrier = pltpu.get_barrier_semaphore()
    for partner in partners:
        pl.semaphore_signal(barrier, inc=1, device_id=partner, device_id_type=MESH)

    @pl.when(here.moves)
    def _():
        for partner in (here.crossed, here.crossed_partner):
            pl.semaphore_signal(barrier, inc=1, device_id=partner, device_id_type=MESH)

    loads = [
        pltpu.make_async_copy(weights.at[:, :, pl.ds(half * WIDE, WIDE)], w[half], in_sem.at[half])
        for half in range(2)
    ]
    loads.append(pltpu.make_async_copy(phase, phase_v, in_sem.at[2]))
    loads.append(pltpu.make_async_copy(ops, ops_v, in_sem.at[3]))
    for load in loads:
        load.start()

    def remote(src, dst, send, recv, target):
        return pltpu.make_async_remote_copy(
            src_ref=src, dst_ref=dst, send_sem=send, recv_sem=recv, device_id=target, device_id_type=MESH
        )

    def other_copy(half, piece):
        rows = pl.ds(piece * PIECE, PIECE)
        target = here.crossed_partner if half == CROSSED else partners[0]
        return remote(
            sent0[half].at[rows], got0[half].at[rows], send0_sem.at[half, piece], recv0_sem.at[half, piece], target
        )

    def kept_copy(piece):
        rows = pl.ds(piece * PIECE, PIECE)
        return remote(
            sent_kept.at[rows], got_kept.at[rows], send0_sem.at[2, piece], recv0_sem.at[2, piece], here.crossed
        )

    def angle_copy():
        return remote(angles_out, angles_in, angle_sem.at[0], angle_sem.at[1], here.crossed)

    def pick(half, side, piece, dst):
        @pl.loop(piece * PIECE, (piece + 1) * PIECE)
        def _(j):
            dst[j] = w[half][slots[0, side * HALF + j]]

    for half in range(2):
        loads[half].wait()
        for piece in range(PIECES):
            pick(half, 1 - sides[0], piece, sent0[half])
            if half == 0 and piece == 0:
                pl.semaphore_wait(barrier, LEVELS + 2 * (here.high + here.low - 2 * here.high * here.low))

            other_copy(half, piece).start()
            if half == CROSSED:

                @pl.when(here.moves)
                def _(piece=piece):
                    pick(CROSSED, sides[0], piece, sent_kept)
                    kept_copy(piece).start()

                @pl.when(jnp.logical_not(here.moves))
                def _(piece=piece):
                    pick(CROSSED, sides[0], piece, got_kept)

    loads[2].wait()
    for level in range(LEVELS - 1):
        angles_out[level] = jnp.concatenate([phase_v[level, :HALF], phase_v[level, HALF:]], axis=1)

    @pl.when(here.moves)
    def _():
        angle_copy().start()

    @pl.when(jnp.logical_not(here.moves))
    def _():
        angles_in[...] = angles_out[...]

    loads[3].wait()
    for level, side, into in (
        (0, sides[0], 0),
        (1, sides[1], 1),
        (2, sides[2], 2),
        (1, sides[3], 3),
        (3, sides[3], None),
        (3, None, None),
    ):
        for c in range(4):
            child = c if side is None else lax.rem(2 * side + c, 4)

            @pl.loop(0, 4)
            def _(q, level=level, side=side, into=into, c=c, child=child):
                real = ops_v[level, q, child, 0]
                imag = ops_v[level, q, child, 1]
                block = jnp.concatenate(
                    [jnp.concatenate([real, -imag], axis=1), jnp.concatenate([imag, real], axis=1)], axis=0
                )
                if into is None:
                    order = CROSSED if side is None else PLAIN
                    matrix[order, pl.ds(q * ROWS, ROWS), pl.ds(c * ROWS, ROWS)] = block
                else:
                    turned[into, q, pl.ds(c * ROWS, ROWS), :] = block.T

    def factors(half, level, angles):
        cos_l, sin_l = jnp.cos(angles), jnp.sin(angles)
        cosine[half, level] = jnp.concatenate([cos_l, cos_l], axis=1)
        sine[half, level] = jnp.concatenate([-sin_l, sin_l], axis=1)

    for level in range(LEVELS - 1):
        factors(PLAIN, level, phase_v[level])
    flat = phase_v[LEVELS - 1].T
    cos_l, sin_l = jnp.cos(flat), jnp.sin(flat)
    for i in range(PAIRS):
        cos3[i] = jnp.broadcast_to(cos_l[:, i : i + 1], (RANK, WIDE))
        sin3[i] = jnp.broadcast_to(sin_l[:, i : i + 1], (RANK, WIDE))

    def rotate(half, level, pair, z):
        c = cosine[half, level, pl.ds(pair, 1), :]
        s = sine[half, level, pl.ds(pair, 1), :]
        return (z * c + pltpu.roll(z, RANK, 1) * s).astype(jnp.bfloat16)

    def mix(which, columns):
        return [
            jnp.dot(columns, turned[which, q], preferred_element_type=jnp.float32) for q in range(4)
        ]

    def first_level(half, piece):
        other_copy(half, piece).wait_recv()
        if half == CROSSED:

            @pl.when(here.moves)
            def _():
                kept_copy(piece).wait_recv()

        @pl.loop(piece * PIECE // 2, (piece + 1) * PIECE // 2, step=2)
        def _(g0):
            stack = []
            for k in range(2):
                g = g0 + k
                if half == CROSSED:
                    tiles = [got_kept[2 * g + e].T for e in range(2)]
                else:
                    tiles = [w[half][slots[0, sides[0] * HALF + 2 * g + e]].T for e in range(2)]
                tiles += [got0[half][2 * g + e].T for e in range(2)]
                stack.append(jnp.concatenate(tiles, axis=1))
            z = mix(0, jnp.concatenate(stack, axis=0))
            for k in range(2):
                for q in range(4):
                    pair = (g0 + k) * 4 + q
                    state[1][pair, pl.ds(half * WIDE, WIDE), :] = rotate(
                        half, 0, pair, z[q][k * WIDE : (k + 1) * WIDE]
                    )

    def hop(level, half):
        return 3 if level == 1 and half == CROSSED else level

    def parts(level, c):
        if level == LEVELS - 1 and c == LAST:
            return [pl.ds(piece * PIECE, PIECE) for piece in range(PIECES)]
        return [pl.ds(0, HALF)]

    def chunk_copy(level, half, c, n):
        rows, at = parts(level, c)[n], hop(level, half)
        return remote(
            sent[level, half, c].at[rows],
            got[level, half, c].at[rows],
            send_sem.at[level - 1, half, c, n],
            recv_sem.at[level - 1, half, c, n],
            partners[at],
        )

    def home_copy(c, n, u, slot):
        rows = parts(LEVELS - 1, c)[n]
        return remote(
            sent[LEVELS - 1, CROSSED, c].at[u, rows],
            got[LEVELS - 1, CROSSED, c].at[slot, rows],
            home_send_sem.at[u, c, n],
            home_recv_sem.at[slot, c, n],
            here.homes[u],
        )

    started = []

    def send(level, half, c):
        if c >= CHUNKS:
            return
        columns = pl.ds(half * WIDE + STARTS[c], WIDTHS[c])

        def gather(side, rows, put):
            @pl.loop(rows.start, rows.start + rows.size, unroll=4)
            def _(j):
                put(j, state[level][slots[level, side * HALF + j], columns, :])

        for n, rows in enumerate(parts(level, c)):
            if level < LEVELS - 1 or half == PLAIN:

                def put(j, tile):
                    sent[level, half, c][j] = tile

                gather(1 - sides[hop(level, half)], rows, put)
                chunk_copy(level, half, c, n).start()
                started.append((level, half, c, n))
                continue
            for u in range(2):

                @pl.when(here.stays(u))
                def _(u=u, rows=rows):
                    def put(j, tile):
                        got[level, half, c][u, j] = tile

                    gather(u, rows, put)

                @pl.when(jnp.logical_not(here.stays(u)))
                def _(u=u, rows=rows, n=n):
                    def put(j, tile):
                        sent[level, half, c][u, j] = tile

                    gather(u, rows, put)
                    home_copy(c, n, u, here.high).start()

    def middle_level(level, half, c):
        width, block = WIDTHS[c], 256 // WIDTHS[c]
        columns = pl.ds(half * WIDE + STARTS[c], width)
        side = sides[hop(level, half)]
        which = 3 if level == 1 and half == CROSSED else level

        @pl.loop(0, GROUPS, step=block)
        def _(g0):
            stack = []
            for k in range(block):
                g = g0 + k
                tiles = [state[level][slots[level, side * HALF + 2 * g + e], columns, :] for e in range(2)]
                tiles += [got[level, half, c][2 * g + e] for e in range(2)]
                stack.append(jnp.concatenate(tiles, axis=1))
            z = mix(which, jnp.concatenate(stack, axis=0))
            for k in range(block):
                for q in range(4):
                    pair = (g0 + k) * 4 + q
                    state[level + 1][pair, columns, :] = rotate(half, level, pair, z[q][k * width : (k + 1) * width])

    stores = []

    def last_level(half, piece):
        level = LEVELS - 1
        for c in range(CHUNKS):
            n = piece if c == LAST else 0
            if c < LAST and piece > 0:
                continue
            if half == PLAIN:
                chunk_copy(level, half, c, n).wait_recv()
                continue
            for s in range(2):

                @pl.when(jnp.logical_not(here.stays(s)))
                def _(c=c, n=n, s=s):
                    home_copy(c, n, 0, s).wait_recv()

        @pl.loop(piece * GROUPS // PIECES, (piece + 1) * GROUPS // PIECES, step=2)
        def _(g0):
            stack = []
            for k in range(2):
                g = g0 + k
                if half == PLAIN:
                    tiles = [
                        state[level][slots[level, sides[level] * HALF + 2 * g + e], pl.ds(half * WIDE, WIDE), :]
                        for e in range(2)
                    ]
                    tiles += [
                        jnp.concatenate([got[level, half, c][2 * g + e] for c in range(CHUNKS)], axis=0)
                        for e in range(2)
                    ]
                else:
                    tiles = [
                        jnp.concatenate([got[level, half, c][s, 2 * g + e] for c in range(CHUNKS)], axis=0)
                        for s in range(2)
                        for e in range(2)
                    ]
                stack.append(jnp.concatenate(tiles, axis=1))
            z = lax.dot_general(
                matrix[half],
                jnp.concatenate(stack, axis=0),
                (((1,), (1,)), ((), ())),
                preferred_element_type=jnp.float32,
            )
            for k in range(2):
                for q in range(4):
                    pair = (g0 + k) * 4 + q
                    lanes = slice(k * WIDE, (k + 1) * WIDE)
                    real = z[q * ROWS : q * ROWS + RANK, lanes]
                    imag = z[q * ROWS + RANK : (q + 1) * ROWS, lanes]
                    c, s = cos3[pair], sin3[pair]
                    result[half][pair, :RANK, :] = (real * c - imag * s).astype(jnp.bfloat16)
                    result[half][pair, RANK:, :] = (real * s + imag * c).astype(jnp.bfloat16)

        pairs = pl.ds(piece * PAIRS // PIECES, PAIRS // PIECES)
        store = pltpu.make_async_copy(
            result[half].at[pairs], out.at[pairs, :, pl.ds(half * WIDE, WIDE)], out_sem.at[half, piece]
        )
        store.start()
        stores.append(store)

    def take(level, half, c):
        chunk_copy(level, half, c, 0).wait_recv()
        if level == 1:
            send(1, half, c + WINDOW)
        middle_level(level, half, c)
        send(level + 1, half, c)

    for piece in range(PIECES):
        first_level(PLAIN, piece)

    @pl.when(here.moves)
    def _():
        angle_copy().wait_recv()

    for level in range(LEVELS - 1):
        packed = angles_in[level]
        factors(CROSSED, level, jnp.concatenate([packed[:, :RANK], packed[:, RANK:]], axis=0))
    for piece in range(PIECES):
        first_level(CROSSED, piece)
        if piece == PIECES - 2:
            for c in range(WINDOW):
                send(1, PLAIN, c)
    for c in range(WINDOW):
        send(1, CROSSED, c)
    for c in range(CHUNKS + LAG):
        if c < CHUNKS:
            take(1, PLAIN, c)
            take(1, CROSSED, c)
        if c >= LAG:
            take(2, PLAIN, c - LAG)
            take(2, CROSSED, c - LAG)
    for piece in range(PIECES):
        last_level(PLAIN, piece)
        last_level(CROSSED, piece)

    for store in stores:
        store.wait()
    for half in range(2):
        for piece in range(PIECES):
            other_copy(half, piece).wait_send()
    for key in started:
        chunk_copy(*key).wait_send()

    @pl.when(here.moves)
    def _():
        angle_copy().wait_send()
        for piece in range(PIECES):
            kept_copy(piece).wait_send()

    for u in range(2):

        @pl.when(jnp.logical_not(here.stays(u)))
        def _(u=u):
            for c in range(CHUNKS):
                for n in range(len(parts(LEVELS - 1, c))):
                    home_copy(c, n, u, 0).wait_send()


def on_device(weights, slot_map, ops, phase):
    hbm = pl.BlockSpec(memory_space=pl.ANY)
    bf16, f32 = jnp.bfloat16, jnp.float32
    scratch = [pltpu.VMEM((PAIRS, ROWS, WIDE), bf16)] * 2
    scratch += [
        pltpu.VMEM(ops.shape, bf16),
        pltpu.VMEM(phase.shape, f32),
        pltpu.VMEM((LEVELS - 1, HALF, ROWS), f32),
        pltpu.VMEM((LEVELS - 1, HALF, ROWS), f32),
        pltpu.VMEM((2, BIG, BIG), bf16),
        pltpu.VMEM((4, 4, BIG, ROWS), bf16),
        pltpu.VMEM((2, LEVELS - 1, PAIRS, ROWS), f32),
        pltpu.VMEM((2, LEVELS - 1, PAIRS, ROWS), f32),
        pltpu.VMEM((PAIRS, RANK, WIDE), f32),
        pltpu.VMEM((PAIRS, RANK, WIDE), f32),
    ]
    scratch += [pltpu.VMEM((PAIRS, SIDES, ROWS), bf16)] * (LEVELS - 1)
    scratch += [pltpu.VMEM((HALF, ROWS, WIDE), bf16)] * 6
    scratch += [pltpu.VMEM((PAIRS, ROWS, WIDE), bf16)] * 2
    for level in range(1, LEVELS):
        for half in range(2):
            for width in WIDTHS:
                shape = (HALF, width, ROWS)
                if level == LEVELS - 1 and half == CROSSED:
                    shape = (2,) + shape
                scratch += [pltpu.VMEM(shape, bf16)] * 2
    scratch += [
        pltpu.SemaphoreType.DMA((4,)),
        pltpu.SemaphoreType.DMA((2, PIECES)),
        pltpu.SemaphoreType.DMA((3, PIECES)),
        pltpu.SemaphoreType.DMA((3, PIECES)),
        pltpu.SemaphoreType.DMA((2,)),
        pltpu.SemaphoreType.DMA((LEVELS - 1, 2, CHUNKS, PIECES)),
        pltpu.SemaphoreType.DMA((LEVELS - 1, 2, CHUNKS, PIECES)),
        pltpu.SemaphoreType.DMA((2, CHUNKS, PIECES)),
        pltpu.SemaphoreType.DMA((2, CHUNKS, PIECES)),
    ]
    out = pl.pallas_call(
        kernel,
        out_shape=jax.ShapeDtypeStruct((PAIRS, ROWS, SIDES), bf16),
        in_specs=[pl.BlockSpec(memory_space=pltpu.SMEM), hbm, hbm, hbm],
        out_specs=hbm,
        scratch_shapes=scratch,
        compiler_params=pltpu.CompilerParams(
            collective_id=0, has_side_effects=True, vmem_limit_bytes=60 * 2**20
        ),
        cost_estimate=pl.CostEstimate(flops=8_600_000_000, bytes_accessed=10_000_000, transcendentals=0),
    )(slot_map, weights.reshape(PAIRS, ROWS, SIDES), ops, phase)
    return out.reshape(weights.shape)


def solution(mesh):
    placed = (P(("gx", "gy"), None, None, None), P(), P(), P(None, ("gx", "gy"), None))
    return jax.shard_map(
        on_device,
        mesh=mesh,
        in_specs=placed,
        out_specs=P(("gx", "gy"), None, None, None),
        check_vma=False,
    )
```
